32 devices in a mesh: node: 4 (over z), dev: 8 (over y, x, core).
Axes of the slice: x: 2, y: 2, z: 4, core: 2. Of those that a mesh axis runs over, the one named last changes fastest.
Arguments:
- tables: bfloat16 [64, 2048, 256], P(('node', 'dev')), may hold values from -0.5 to 0.5
- ids: int32 [64, 512, 8], P(None, ('node', 'dev')), may hold values from 0 to 2047
- counts: int32 [64, 32], P(('node', 'dev')), may hold values from 1 to 12, as said below
Outputs:
- interaction: bfloat16 [512, 64, 64], P(('node', 'dev'))
The draws below stay inside these ranges and needn't reach their ends.
Inputs may be any that keep to these rules, and one draw needn't show every extreme that they name: `counts`: every owner has some feature with exactly 12 live samples, and each feature reaches 12 for some owner. `ids`: row indices may be packed several to a word wherever they travel.
All inputs are finite; a program needn't handle non-finite values.
Results may differ from the reference program's by a relative error of at most 0.0049.
Values may be sent and summed in bfloat16 or wider, within the bound.
A program may use at most 64 MiB of HBM per device.

```python
import jax
import jax.numpy as jnp
from jax import lax

D = 256
ROWS = 2048
BAG = 8
F_DEV = 2
B_DEV = 16
LIVE = 12
FEATURES = 64
BATCH = 512


def draw_counts(key, part):
    first, second, third = jax.random.split(jax.random.fold_in(key, 11), 3)
    owners = FEATURES // F_DEV
    base = jax.random.randint(first, (FEATURES, owners), 1, LIVE + 1)
    lottery = jax.random.randint(third, (FEATURES, owners), 0, 4)
    filled = jnp.where(lottery == 0, base, LIVE)
    picked = jax.random.randint(second, (owners,), 0, FEATURES)
    feature_rows = lax.broadcasted_iota(jnp.int32, (FEATURES, owners), 0)
    forced = jnp.where(feature_rows == picked[None, :], LIVE, filled)
    diagonal = lax.broadcasted_iota(jnp.int32, (FEATURES, owners), 1) == feature_rows % owners
    return jnp.where(diagonal, LIVE, forced).astype(jnp.int32)


def set_ends(values, own_key, low, high):
    place = [jax.random.randint(jax.random.fold_in(own_key, axis), (), 0, length) for axis, length in enumerate(values.shape)]
    widest = values.shape.index(max(values.shape))
    neighbour = place[:widest] + [(place[widest] + 1) % values.shape[widest]] + place[widest + 1:]
    return values.at[tuple(place)].set(low).at[tuple(neighbour)].set(high)


def block_scale(rng, dims, cuts, least, top_value):
    loudness = 1.0
    for dim, parts in cuts:
        heights = jax.random.uniform(jax.random.fold_in(jax.random.fold_in(rng, 6), dim), (parts,), jnp.float32, least / len(cuts), top_value / len(cuts))
        loudness = loudness * jnp.repeat(jnp.exp(heights), dims[dim] // parts).reshape((-1,) + (1,) * (len(dims) - 1 - dim))
    return loudness


def gaussian(key, shape, spread, most, pieces=(), kind=jnp.bfloat16):
    array = spread * jax.random.normal(key, shape, jnp.float32)
    if pieces:
        array = array * block_scale(key, shape, pieces, -0.22, 0.18)
    return jnp.clip(array, -most, most).astype(kind)


def setup_inputs(seed: int = 0) -> dict:
    streams_of = jax.random.split(jax.random.key(seed), 4)
    return {
        "tables": gaussian(streams_of[0], (FEATURES, ROWS, D), 0.0625, 0.5, ((0, 32),)),
        "ids": set_ends(jax.random.randint(streams_of[1], (FEATURES, BATCH, BAG), 0, ROWS), jax.random.fold_in(streams_of[1], 1), 0, ROWS - 1).astype(jnp.int32),
        "counts": draw_counts(jax.random.fold_in(streams_of[3], 71), 0),
    }


def pool_table(pair):
    table, index = pair
    rows = table[index].astype(jnp.float32)
    return jnp.sum(rows, axis=1).astype(jnp.bfloat16)


def gram_block(block):
    values = block.astype(jnp.float32)
    return jnp.einsum("fsd,gsd->sfg", values, values).astype(jnp.bfloat16)


def reference(tables, ids, counts):
    pooled = lax.map(pool_table, (tables, ids))
    total = ids.shape[1]
    position = jnp.arange(total, dtype=jnp.int32)
    local = position % B_DEV
    owner = position // B_DEV
    live = local[None, :] < counts[:, owner]
    masked = jnp.where(live[:, :, None], pooled, jnp.zeros_like(pooled))
    blocks = masked.reshape(FEATURES, total // B_DEV, B_DEV, D)
    blocks = jnp.moveaxis(blocks, 1, 0)
    grams = lax.map(gram_block, blocks)
    return grams.reshape(total, FEATURES, FEATURES)
```

```python
import functools

import jax
import jax.numpy as jnp
from jax import lax
from jax.experimental import pallas as pl
from jax.experimental.pallas import tpu as pltpu
from jax.sharding import PartitionSpec as P

LIVE = 12
LANES = 128
MESH = pl.DeviceIdType.MESH


def kernel(
    groups, members, owned, bagged,
    table_ref, ids_ref, counts_ref, out_ref,
    id_got, tally, staged, outgoing, received, vectors,
    id_send, id_recv, row_send, row_recv,
):
    total = groups * members
    held, height, width = table_ref.shape
    halves = width // LANES
    lines = held * halves * LIVE
    node = lax.axis_index("node")
    dev = lax.axis_index("dev")
    me = node * members + dev

    def place(device):
        return (device // members, lax.rem(device, members))

    def id_copy(device, source):
        return pltpu.make_async_remote_copy(
            src_ref=ids_ref.at[device],
            dst_ref=id_got.at[source],
            send_sem=id_send.at[device],
            recv_sem=id_recv.at[source],
            device_id=place(device),
            device_id_type=MESH,
        )

    def row_copy(device, source):
        return pltpu.make_async_remote_copy(
            src_ref=outgoing.at[device],
            dst_ref=received.at[source],
            send_sem=row_send.at[device],
            recv_sem=row_recv.at[source],
            device_id=place(device),
            device_id_type=MESH,
        )

    barrier = pltpu.get_barrier_semaphore()

    @pl.loop(1, total)
    def _(step):
        pl.semaphore_signal(
            barrier, inc=1, device_id=place(lax.rem(me + step, total)), device_id_type=MESH
        )

    pl.semaphore_wait(barrier, total - 1)

    @pl.loop(1, total)
    def _(step):
        id_copy(lax.rem(me + step, total), me).start()

    id_got[me] = ids_ref[me]

    spread = (
        lax.rem(lax.broadcasted_iota(jnp.int32, (2 * LANES, bagged * LANES), 0), bagged)
        == lax.broadcasted_iota(jnp.int32, (2 * LANES, bagged * LANES), 1) // LANES
    ).astype(jnp.float32).astype(jnp.bfloat16)
    sample = lax.broadcasted_iota(jnp.int32, (LIVE, members, LANES), 0)
    on_lane = lax.broadcasted_iota(jnp.int32, (LIVE, members, LANES), 2) // bagged == sample
    rows = LIVE * members

    for turn in range(groups):
        group = lax.rem(node + turn + 1, groups)
        first = group * members

        def wait_ids(member):
            id_copy(first + member, first + member).wait_recv()

        if turn < groups - 1:
            @pl.loop(0, members)
            def _(member):
                wait_ids(member)
        else:
            @pl.loop(1, members)
            def _(step):
                wait_ids(lax.rem(dev + step, members))

        for feature in range(held):
            index = id_got[pl.ds(first, members), feature, :]
            high = jnp.where(on_lane, (index - (index & 15))[None], 0)
            low = jnp.where(on_lane, (index & 15)[None], 0)
            both = jnp.concatenate(
                [high.reshape(rows, LANES), low.reshape(rows, LANES)], axis=1
            ).astype(jnp.float32).astype(jnp.bfloat16)
            wide = jnp.dot(both, spread, preferred_element_type=jnp.float32)
            wide = wide.astype(jnp.int32).astype(jnp.int16)
            number = lax.broadcasted_iota(jnp.int32, (16, height), 1).astype(jnp.int16)
            for part in range(rows // 16):
                count = jnp.zeros((16, height), jnp.bfloat16)
                for entry in range(bagged):
                    piece = wide[part * 16:(part + 1) * 16, entry * LANES:(entry + 1) * LANES]
                    piece = jnp.concatenate([piece] * (height // LANES), axis=1)
                    count = count + jnp.where(
                        piece == number, jnp.ones((), jnp.bfloat16), jnp.zeros((), jnp.bfloat16)
                    )
                tally[part * 16:(part + 1) * 16, :] = count
            pooled = jnp.dot(
                tally[...], table_ref[feature], preferred_element_type=jnp.float32
            )
            limit = counts_ref[pl.ds(first, members), feature, :]
            for half in range(halves):
                for s in range(LIVE):
                    piece = pooled[s * members:(s + 1) * members, half * LANES:(half + 1) * LANES]
                    line = (feature * halves + half) * LIVE + s
                    staged[pl.ds(line, members, stride=lines), :] = jnp.where(s < limit, piece, 0.0)
        outgoing[pl.ds(first, members)] = (
            staged[...].reshape(members, lines, LANES).astype(jnp.bfloat16)
        )

        if turn < groups - 1:
            @pl.loop(0, members)
            def _(step):
                row_copy(first + lax.rem(dev + step, members), me).start()
        else:
            @pl.loop(1, members)
            def _(step):
                row_copy(first + lax.rem(dev + step, members), me).start()

    received[me] = outgoing[me]
    out_ref[LIVE:] = jnp.zeros_like(out_ref[LIVE:])

    for turn in range(groups):
        group = lax.rem(node + 2 * groups - turn - 1, groups)
        first = group * members
        if turn < groups - 1:
            @pl.loop(0, members)
            def _(member):
                row_copy(first + member, first + member).wait_recv()
        else:
            @pl.loop(1, members)
            def _(step):
                source = first + lax.rem(dev + step, members)
                row_copy(source, source).wait_recv()
        staged[...] = (
            received[pl.ds(first, members)].astype(jnp.float32).reshape(members * lines, LANES)
        )
        for feature in range(held):
            for half in range(halves):
                for s in range(LIVE):
                    line = (feature * halves + half) * LIVE + s
                    vectors[s, half, group, pl.ds(feature, members, stride=held), :] = (
                        staged[pl.ds(line, members, stride=lines), :]
                    )

    for s in range(LIVE):
        mine = jnp.concatenate(
            [vectors[s, half].reshape(total * held, LANES) for half in range(halves)], axis=1
        ).astype(jnp.bfloat16)
        out_ref[s] = lax.dot_general(
            mine, mine, (((1,), (1,)), ((), ())), preferred_element_type=jnp.float32
        ).astype(jnp.bfloat16)

    @pl.loop(1, total)
    def _(step):
        device = lax.rem(me + step, total)
        id_copy(device, me).wait_send()
        row_copy(device, me).wait_send()


def shards(tables, ids, counts):
    held, height, width = tables.shape
    features, owned, bagged = ids.shape
    groups = lax.axis_size("node")
    members = lax.axis_size("dev")
    total = groups * members
    lines = held * (width // LANES) * LIVE
    index = ids.reshape(total, held, owned * bagged)
    limits = jnp.broadcast_to(counts.T[:, :, None], (total, held, LANES))
    return pl.pallas_call(
        functools.partial(kernel, groups, members, owned, bagged),
        out_shape=jax.ShapeDtypeStruct((owned, features, features), jnp.bfloat16),
        in_specs=[pl.BlockSpec(memory_space=pltpu.VMEM)] * 3,
        out_specs=pl.BlockSpec(memory_space=pltpu.VMEM),
        scratch_shapes=[
            pltpu.VMEM((total, held, LANES), jnp.int32),
            pltpu.VMEM((LIVE * members, height), jnp.bfloat16),
            pltpu.VMEM((members * lines, LANES), jnp.float32),
            pltpu.VMEM((total, lines, LANES), jnp.bfloat16),
            pltpu.VMEM((total, lines, LANES), jnp.bfloat16),
            pltpu.VMEM((LIVE, width // LANES, groups, members * held, LANES), jnp.float32),
            pltpu.SemaphoreType.DMA((total,)),
            pltpu.SemaphoreType.DMA((total,)),
            pltpu.SemaphoreType.DMA((total,)),
            pltpu.SemaphoreType.DMA((total,)),
        ],
        compiler_params=pltpu.CompilerParams(
            collective_id=0, has_side_effects=True, vmem_limit_bytes=48 * 1024 * 1024
        ),
    )(tables, index, limits)


def solution(mesh):
    return jax.shard_map(
        shards,
        mesh=mesh,
        in_specs=(
            P(("node", "dev"), None, None),
            P(None, ("node", "dev"), None),
            P(("node", "dev"), None),
        ),
        out_specs=P(("node", "dev"), None, None),
        check_vma=False,
    )
```

```python
import functools

import jax
import jax.numpy as jnp
from jax import lax
from jax.experimental import pallas as pl
from jax.experimental.pallas import tpu as pltpu
from jax.sharding import PartitionSpec as P

LIVE = 12
LANES = 128
MESH = pl.DeviceIdType.MESH


def kernel(
    groups, members, owned, bagged,
    table_hbm, ids_hbm, counts_hbm, out_ref,
    table_ref, ids_in, counts_in, ids_ref, limits,
    id_got, tally, staged, outgoing, received, vectors,
    table_sem, ids_sem, counts_sem, id_send, id_recv, row_send, row_recv,
):
    total = groups * members
    held, height, width = table_ref.shape
    if groups & (groups - 1):
        turns = [None] * groups
    else:
        turns, bit = [], groups // 2
        while bit:
            turns += list(range(bit, 2 * bit))
            bit //= 2
        turns.append(0)
    halves = width // LANES
    lines = held * halves * LIVE
    node = lax.axis_index("node")
    dev = lax.axis_index("dev")
    me = node * members + dev

    def place(device):
        return (device // members, lax.rem(device, members))

    def id_copy(device, source):
        return pltpu.make_async_remote_copy(
            src_ref=ids_ref.at[device],
            dst_ref=id_got.at[source],
            send_sem=id_send.at[device],
            recv_sem=id_recv.at[source],
            device_id=place(device),
            device_id_type=MESH,
        )

    def row_copy(device, source):
        return pltpu.make_async_remote_copy(
            src_ref=outgoing.at[device],
            dst_ref=received.at[source],
            send_sem=row_send.at[device],
            recv_sem=row_recv.at[source],
            device_id=place(device),
            device_id_type=MESH,
        )

    load_ids = pltpu.make_async_copy(ids_hbm, ids_in, ids_sem)
    load_counts = pltpu.make_async_copy(counts_hbm, counts_in, counts_sem)
    load_tables = pltpu.make_async_copy(table_hbm, table_ref, table_sem)
    load_ids.start()
    load_counts.start()
    load_tables.start()

    def partner(turn):
        mask = turns[turn]
        if mask is None:
            return lax.rem(node + turn + 1, groups)
        other, bit = 0, 1
        while bit < groups:
            digit = lax.rem(node // bit, 2)
            other = other + bit * (1 - digit if mask & bit else digit)
            bit *= 2
        return other

    def origin(turn):
        if turns[turn] is None:
            return lax.rem(node + 2 * groups - turn - 1, groups)
        return partner(turn)

    barrier = pltpu.get_barrier_semaphore()

    @pl.loop(1, total)
    def _(step):
        pl.semaphore_signal(
            barrier, inc=1, device_id=place(lax.rem(me + step, total)), device_id_type=MESH
        )

    load_ids.wait()
    turned = ids_in[...].T
    for device in range(total):
        ids_ref[device] = turned[device * held:(device + 1) * held, :]

    pl.semaphore_wait(barrier, total - 1)

    @pl.loop(1, total)
    def _(step):
        id_copy(lax.rem(me + step, total), me).start()

    id_got[me] = ids_ref[me]

    spread = (
        lax.rem(lax.broadcasted_iota(jnp.int32, (2 * LANES, bagged * LANES), 0), bagged)
        == lax.broadcasted_iota(jnp.int32, (2 * LANES, bagged * LANES), 1) // LANES
    ).astype(jnp.float32).astype(jnp.bfloat16)
    sample = lax.broadcasted_iota(jnp.int32, (LIVE, members, LANES), 0)
    on_lane = lax.broadcasted_iota(jnp.int32, (LIVE, members, LANES), 2) // bagged == sample
    rows = LIVE * members

    load_counts.wait()
    square = (total, total)
    diagonal = lax.broadcasted_iota(jnp.int32, square, 0) == lax.broadcasted_iota(jnp.int32, square, 1)
    for feature in range(held):
        level = counts_in[feature:feature + 1, :].astype(jnp.float32)
        column = jnp.sum(jnp.where(diagonal, level, 0.0), axis=1, keepdims=True)
        limits[feature] = jnp.broadcast_to(column, (total, LANES))

    for turn in range(groups):
        group = partner(turn)
        first = group * members

        def wait_ids(member):
            id_copy(first + member, first + member).wait_recv()

        if turn < groups - 1:
            @pl.loop(0, members)
            def _(member):
                wait_ids(member)
        else:
            @pl.loop(1, members)
            def _(step):
                wait_ids(lax.rem(dev + step, members))

        for feature in range(held):
            index = id_got[pl.ds(first, members), feature, :]
            high = jnp.where(on_lane, (index - (index & 15))[None], 0)
            low = jnp.where(on_lane, (index & 15)[None], 0)
            both = jnp.concatenate(
                [high.reshape(rows, LANES), low.reshape(rows, LANES)], axis=1
            ).astype(jnp.float32).astype(jnp.bfloat16)
            wide = jnp.dot(both, spread, preferred_element_type=jnp.float32)
            wide = wide.astype(jnp.int32).astype(jnp.int16)
            number = lax.broadcasted_iota(jnp.int32, (16, height), 1).astype(jnp.int16)
            for part in range(rows // 16):
                count = jnp.zeros((16, height), jnp.bfloat16)
                for entry in range(bagged):
                    piece = wide[part * 16:(part + 1) * 16, entry * LANES:(entry + 1) * LANES]
                    piece = jnp.concatenate([piece] * (height // LANES), axis=1)
                    count = count + jnp.where(
                        piece == number, jnp.ones((), jnp.bfloat16), jnp.zeros((), jnp.bfloat16)
                    )
                tally[part * 16:(part + 1) * 16, :] = count
            if turn == 0 and feature == 0:
                load_tables.wait()
            pooled = jnp.dot(
                tally[...], table_ref[feature], preferred_element_type=jnp.float32
            )
            limit = limits[feature, pl.ds(first, members), :]
            for half in range(halves):
                for s in range(LIVE):
                    piece = pooled[s * members:(s + 1) * members, half * LANES:(half + 1) * LANES]
                    line = (feature * halves + half) * LIVE + s
                    staged[pl.ds(line, members, stride=lines), :] = jnp.where(s < limit, piece, 0.0)
        outgoing[pl.ds(first, members)] = (
            staged[...].reshape(members, lines, LANES).astype(jnp.bfloat16)
        )

        if turn < groups - 1:
            @pl.loop(0, members)
            def _(step):
                row_copy(first + lax.rem(dev + step, members), me).start()
        else:
            @pl.loop(1, members)
            def _(step):
                row_copy(first + lax.rem(dev + step, members), me).start()

    received[me] = outgoing[me]
    out_ref[LIVE:] = jnp.zeros_like(out_ref[LIVE:])

    for turn in range(groups):
        group = origin(turn)
        first = group * members
        if turn < groups - 1:
            @pl.loop(0, members)
            def _(member):
                row_copy(first + member, first + member).wait_recv()
        else:
            @pl.loop(1, members)
            def _(step):
                source = first + lax.rem(dev + step, members)
                row_copy(source, source).wait_recv()
        staged[...] = (
            received[pl.ds(first, members)].astype(jnp.float32).reshape(members * lines, LANES)
        )
        for feature in range(held):
            for half in range(halves):
                for s in range(LIVE):
                    line = (feature * halves + half) * LIVE + s
                    vectors[s, half, group, pl.ds(feature, members, stride=held), :] = (
                        staged[pl.ds(line, members, stride=lines), :]
                    )

    for s in range(LIVE):
        mine = jnp.concatenate(
            [vectors[s, half].reshape(total * held, LANES) for half in range(halves)], axis=1
        ).astype(jnp.bfloat16)
        out_ref[s] = lax.dot_general(
            mine, mine, (((1,), (1,)), ((), ())), preferred_element_type=jnp.float32
        ).astype(jnp.bfloat16)

    @pl.loop(1, total)
    def _(step):
        device = lax.rem(me + step, total)
        id_copy(device, me).wait_send()
        row_copy(device, me).wait_send()


def shards(tables, ids, counts):
    held, height, width = tables.shape
    features, owned, bagged = ids.shape
    groups = lax.axis_size("node")
    members = lax.axis_size("dev")
    total = groups * members
    lines = held * (width // LANES) * LIVE
    index = ids.transpose(1, 2, 0).reshape(owned * bagged, features)
    return pl.pallas_call(
        functools.partial(kernel, groups, members, owned, bagged),
        out_shape=jax.ShapeDtypeStruct((owned, features, features), jnp.bfloat16),
        in_specs=[pl.BlockSpec(memory_space=pltpu.HBM)] * 3,
        out_specs=pl.BlockSpec(memory_space=pltpu.VMEM),
        scratch_shapes=[
            pltpu.VMEM(tables.shape, tables.dtype),
            pltpu.VMEM(index.shape, index.dtype),
            pltpu.VMEM(counts.shape, counts.dtype),
            pltpu.VMEM((total, held, LANES), jnp.int32),
            pltpu.VMEM((held, total, LANES), jnp.float32),
            pltpu.VMEM((total, held, LANES), jnp.int32),
            pltpu.VMEM((LIVE * members, height), jnp.bfloat16),
            pltpu.VMEM((members * lines, LANES), jnp.float32),
            pltpu.VMEM((total, lines, LANES), jnp.bfloat16),
            pltpu.VMEM((total, lines, LANES), jnp.bfloat16),
            pltpu.VMEM((LIVE, width // LANES, groups, members * held, LANES), jnp.float32),
            pltpu.SemaphoreType.DMA,
            pltpu.SemaphoreType.DMA,
            pltpu.SemaphoreType.DMA,
            pltpu.SemaphoreType.DMA((total,)),
            pltpu.SemaphoreType.DMA((total,)),
            pltpu.SemaphoreType.DMA((total,)),
            pltpu.SemaphoreType.DMA((total,)),
        ],
        compiler_params=pltpu.CompilerParams(
            collective_id=0, has_side_effects=True, vmem_limit_bytes=64512 * 1024
        ),
    )(tables, index, counts)


def solution(mesh):
    return jax.shard_map(
        shards,
        mesh=mesh,
        in_specs=(
            P(("node", "dev"), None, None),
            P(None, ("node", "dev"), None),
            P(("node", "dev"), None),
        ),
        out_specs=P(("node", "dev"), None, None),
        check_vma=False,
    )
```

```python
import functools

import jax
import jax.numpy as jnp
from jax import lax
from jax.experimental import pallas as pl
from jax.experimental.pallas import tpu as pltpu
from jax.sharding import PartitionSpec as P

LIVE = 12
LANES = 128
MESH = pl.DeviceIdType.MESH


def kernel(
    groups, members, owned, bagged,
    table_hbm, ids_hbm, counts_hbm, out_ref,
    table_ref, ids_in, counts_in, ids_ref, limits,
    id_got, tally, staged, outgoing, received, vectors,
    table_sem, ids_sem, counts_sem, id_send, id_recv, row_send, row_recv,
):
    total = groups * members
    held, height, width = table_ref.shape
    if groups & (groups - 1):
        turns = [None] * groups
    else:
        turns, bit = [], groups // 2
        while bit:
            turns += list(range(bit, 2 * bit))
            bit //= 2
        turns.append(0)
    halves = width // LANES
    lines = held * halves * LIVE
    node = lax.axis_index("node")
    dev = lax.axis_index("dev")
    me = node * members + dev

    def place(device):
        return (device // members, lax.rem(device, members))

    def id_copy(device, source):
        return pltpu.make_async_remote_copy(
            src_ref=ids_ref.at[device],
            dst_ref=id_got.at[source],
            send_sem=id_send.at[device],
            recv_sem=id_recv.at[source],
            device_id=place(device),
            device_id_type=MESH,
        )

    def row_copy(device, source):
        return pltpu.make_async_remote_copy(
            src_ref=outgoing.at[device],
            dst_ref=received.at[source],
            send_sem=row_send.at[device],
            recv_sem=row_recv.at[source],
            device_id=place(device),
            device_id_type=MESH,
        )

    load_ids = pltpu.make_async_copy(ids_hbm, ids_in, ids_sem)
    load_counts = pltpu.make_async_copy(counts_hbm, counts_in, counts_sem)
    load_tables = pltpu.make_async_copy(table_hbm, table_ref, table_sem)
    load_ids.start()
    load_counts.start()
    load_tables.start()

    def partner(turn):
        mask = turns[turn]
        if mask is None:
            return lax.rem(node + turn + 1, groups)
        other, bit = 0, 1
        while bit < groups:
            digit = lax.rem(node // bit, 2)
            other = other + bit * (1 - digit if mask & bit else digit)
            bit *= 2
        return other

    def origin(turn):
        if turns[turn] is None:
            return lax.rem(node + 2 * groups - turn - 1, groups)
        return partner(turn)

    barrier = pltpu.get_barrier_semaphore()

    @pl.loop(1, total)
    def _(step):
        pl.semaphore_signal(
            barrier, inc=1, device_id=place(lax.rem(me + step, total)), device_id_type=MESH
        )

    load_ids.wait()
    turned = ids_in[...].T
    for device in range(total):
        ids_ref[device] = turned[device * held:(device + 1) * held, :]

    pl.semaphore_wait(barrier, total - 1)

    for turn in range(groups):
        begin = partner(turn) * members

        @pl.loop(1 if turn == groups - 1 else 0, members, unroll=True)
        def _(step):
            id_copy(begin + lax.rem(dev + step, members), me).start()

    id_got[me] = ids_ref[me]

    spread = (
        lax.rem(lax.broadcasted_iota(jnp.int32, (2 * LANES, bagged * LANES), 0), bagged)
        == lax.broadcasted_iota(jnp.int32, (2 * LANES, bagged * LANES), 1) // LANES
    ).astype(jnp.float32).astype(jnp.bfloat16)
    sample = lax.broadcasted_iota(jnp.int32, (LIVE, members, LANES), 0)
    on_lane = lax.broadcasted_iota(jnp.int32, (LIVE, members, LANES), 2) // bagged == sample
    rows = LIVE * members

    load_counts.wait()
    square = (total, total)
    diagonal = lax.broadcasted_iota(jnp.int32, square, 0) == lax.broadcasted_iota(jnp.int32, square, 1)
    for feature in range(held):
        level = counts_in[feature:feature + 1, :].astype(jnp.float32)
        column = jnp.sum(jnp.where(diagonal, level, 0.0), axis=1, keepdims=True)
        limits[feature] = jnp.broadcast_to(column, (total, LANES))

    for turn in range(groups):
        group = partner(turn)
        first = group * members

        def wait_ids(member):
            id_copy(first + member, first + member).wait_recv()

        if turn < groups - 1:
            @pl.loop(0, members, unroll=True)
            def _(member):
                wait_ids(member)
        else:
            @pl.loop(1, members, unroll=True)
            def _(step):
                wait_ids(lax.rem(dev + step, members))

        for feature in range(held):
            index = id_got[pl.ds(first, members), feature, :]
            high = jnp.where(on_lane, (index - (index & 15))[None], 0)
            low = jnp.where(on_lane, (index & 15)[None], 0)
            both = jnp.concatenate(
                [high.reshape(rows, LANES), low.reshape(rows, LANES)], axis=1
            ).astype(jnp.float32).astype(jnp.bfloat16)
            wide = jnp.dot(both, spread, preferred_element_type=jnp.float32)
            wide = wide.astype(jnp.int32).astype(jnp.int16)
            number = lax.broadcasted_iota(jnp.int32, (16, height), 1).astype(jnp.int16)
            for part in range(rows // 16):
                count = jnp.zeros((16, height), jnp.bfloat16)
                for entry in range(bagged):
                    piece = wide[part * 16:(part + 1) * 16, entry * LANES:(entry + 1) * LANES]
                    piece = jnp.concatenate([piece] * (height // LANES), axis=1)
                    count = count + jnp.where(
                        piece == number, jnp.ones((), jnp.bfloat16), jnp.zeros((), jnp.bfloat16)
                    )
                tally[part * 16:(part + 1) * 16, :] = count
            if turn == 0 and feature == 0:
                load_tables.wait()
            pooled = jnp.dot(
                tally[...], table_ref[feature], preferred_element_type=jnp.float32
            )
            limit = limits[feature, pl.ds(first, members), :]
            for half in range(halves):
                for s in range(LIVE):
                    piece = pooled[s * members:(s + 1) * members, half * LANES:(half + 1) * LANES]
                    line = (feature * halves + half) * LIVE + s
                    staged[pl.ds(line, members, stride=lines), :] = jnp.where(s < limit, piece, 0.0)
        outgoing[pl.ds(first, members)] = (
            staged[...].reshape(members, lines, LANES).astype(jnp.bfloat16)
        )

        if turn < groups - 1:
            @pl.loop(0, members, unroll=True)
            def _(step):
                row_copy(first + lax.rem(dev + step, members), me).start()
        else:
            @pl.loop(1, members, unroll=True)
            def _(step):
                row_copy(first + lax.rem(dev + step, members), me).start()

    received[me] = outgoing[me]
    out_ref[LIVE:] = jnp.zeros_like(out_ref[LIVE:])

    for turn in range(groups):
        group = origin(turn)
        first = group * members
        if turn < groups - 1:
            @pl.loop(0, members, unroll=True)
            def _(member):
                row_copy(first + member, first + member).wait_recv()
        else:
            @pl.loop(1, members, unroll=True)
            def _(step):
                source = first + lax.rem(dev + step, members)
                row_copy(source, source).wait_recv()
        staged[...] = (
            received[pl.ds(first, members)].astype(jnp.float32).reshape(members * lines, LANES)
        )
        for feature in range(held):
            for half in range(halves):
                for s in range(LIVE):
                    line = (feature * halves + half) * LIVE + s
                    vectors[s, half, group, pl.ds(feature, members, stride=held), :] = (
                        staged[pl.ds(line, members, stride=lines), :]
                    )

    for s in range(LIVE):
        mine = jnp.concatenate(
            [vectors[s, half].reshape(total * held, LANES) for half in range(halves)], axis=1
        ).astype(jnp.bfloat16)
        out_ref[s] = lax.dot_general(
            mine, mine, (((1,), (1,)), ((), ())), preferred_element_type=jnp.float32
        ).astype(jnp.bfloat16)

    @pl.loop(1, total)
    def _(step):
        device = lax.rem(me + step, total)
        id_copy(device, me).wait_send()
        row_copy(device, me).wait_send()


def shards(tables, ids, counts):
    held, height, width = tables.shape
    features, owned, bagged = ids.shape
    groups = lax.axis_size("node")
    members = lax.axis_size("dev")
    total = groups * members
    lines = held * (width // LANES) * LIVE
    index = ids.transpose(1, 2, 0).reshape(owned * bagged, features)
    return pl.pallas_call(
        functools.partial(kernel, groups, members, owned, bagged),
        out_shape=jax.ShapeDtypeStruct((owned, features, features), jnp.bfloat16),
        in_specs=[pl.BlockSpec(memory_space=pltpu.HBM)] * 3,
        out_specs=pl.BlockSpec(memory_space=pltpu.VMEM),
        scratch_shapes=[
            pltpu.VMEM(tables.shape, tables.dtype),
            pltpu.VMEM(index.shape, index.dtype),
            pltpu.VMEM(counts.shape, counts.dtype),
            pltpu.VMEM((total, held, LANES), jnp.int32),
            pltpu.VMEM((held, total, LANES), jnp.float32),
            pltpu.VMEM((total, held, LANES), jnp.int32),
            pltpu.VMEM((LIVE * members, height), jnp.bfloat16),
            pltpu.VMEM((members * lines, LANES), jnp.float32),
            pltpu.VMEM((total, lines, LANES), jnp.bfloat16),
            pltpu.VMEM((total, lines, LANES), jnp.bfloat16),
            pltpu.VMEM((LIVE, width // LANES, groups, members * held, LANES), jnp.float32),
            pltpu.SemaphoreType.DMA,
            pltpu.SemaphoreType.DMA,
            pltpu.SemaphoreType.DMA,
            pltpu.SemaphoreType.DMA((total,)),
            pltpu.SemaphoreType.DMA((total,)),
            pltpu.SemaphoreType.DMA((total,)),
            pltpu.SemaphoreType.DMA((total,)),
        ],
        compiler_params=pltpu.CompilerParams(
            collective_id=0, has_side_effects=True, vmem_limit_bytes=48 * 1024 * 1024
        ),
    )(*(pltpu.with_memory_space_constraint(x, pltpu.HBM) for x in (tables, index, counts)))


def solution(mesh):
    return jax.shard_map(
        shards,
        mesh=mesh,
        in_specs=(
            P(("node", "dev"), None, None),
            P(None, ("node", "dev"), None),
            P(("node", "dev"), None),
        ),
        out_specs=P(("node", "dev"), None, None),
        check_vma=False,
    )
```

```python
import functools

import jax
import jax.numpy as jnp
from jax import lax
from jax.experimental import pallas as pl
from jax.experimental.pallas import tpu as pltpu
from jax.sharding import PartitionSpec as P

LIVE = 12
LANES = 128
MESH = pl.DeviceIdType.MESH


def kernel(
    groups, members, owned, bagged,
    table_hbm, ids_hbm, counts_hbm, out_ref,
    table_ref, ids_in, counts_in, ids_ref, limits,
    id_got, tally, staged, outgoing, received, vectors,
    table_sem, ids_sem, counts_sem, id_send, id_recv, row_send, row_recv,
):
    total = groups * members
    held, height, width = table_ref.shape
    if groups & (groups - 1):
        turns = [None] * groups
    else:
        turns, bit = [], groups // 2
        while bit:
            turns += list(range(bit, 2 * bit))
            bit //= 2
        turns.append(0)
    halves = width // LANES
    lines = held * halves * LIVE
    node = lax.axis_index("node")
    dev = lax.axis_index("dev")
    me = node * members + dev

    def place(device):
        return (device // members, lax.rem(device, members))

    def id_copy(device, source):
        return pltpu.make_async_remote_copy(
            src_ref=ids_ref.at[device],
            dst_ref=id_got.at[source],
            send_sem=id_send.at[device],
            recv_sem=id_recv.at[source],
            device_id=place(device),
            device_id_type=MESH,
        )

    def row_copy(device, source):
        return pltpu.make_async_remote_copy(
            src_ref=outgoing.at[device],
            dst_ref=received.at[source],
            send_sem=row_send.at[device],
            recv_sem=row_recv.at[source],
            device_id=place(device),
            device_id_type=MESH,
        )

    load_ids = pltpu.make_async_copy(ids_hbm, ids_in, ids_sem)
    load_counts = pltpu.make_async_copy(counts_hbm, counts_in, counts_sem)
    load_tables = pltpu.make_async_copy(table_hbm, table_ref, table_sem)
    load_ids.start()
    load_counts.start()
    load_tables.start()

    def partner(turn):
        mask = turns[turn]
        if mask is None:
            return lax.rem(node + turn + 1, groups)
        other, bit = 0, 1
        while bit < groups:
            digit = lax.rem(node // bit, 2)
            other = other + bit * (1 - digit if mask & bit else digit)
            bit *= 2
        return other

    def origin(turn):
        if turns[turn] is None:
            return lax.rem(node + 2 * groups - turn - 1, groups)
        return partner(turn)

    barrier = pltpu.get_barrier_semaphore()

    @pl.loop(1, total)
    def _(step):
        pl.semaphore_signal(
            barrier, inc=1, device_id=place(lax.rem(me + step, total)), device_id_type=MESH
        )

    load_ids.wait()
    turned = ids_in[...].T
    for device in range(total):
        ids_ref[device] = turned[device * held:(device + 1) * held, :]

    pl.semaphore_wait(barrier, total - 1)

    for turn in range(groups):
        begin = partner(turn) * members

        @pl.loop(1 if turn == groups - 1 else 0, members, unroll=True)
        def _(step):
            id_copy(begin + lax.rem(dev + step, members), me).start()

    id_got[me] = ids_ref[me]

    spread = (
        lax.rem(lax.broadcasted_iota(jnp.int32, (2 * LANES, bagged * LANES), 0), bagged)
        == lax.broadcasted_iota(jnp.int32, (2 * LANES, bagged * LANES), 1) // LANES
    ).astype(jnp.float32).astype(jnp.bfloat16)
    sample = lax.broadcasted_iota(jnp.int32, (LIVE, members, LANES), 0)
    on_lane = lax.broadcasted_iota(jnp.int32, (LIVE, members, LANES), 2) // bagged == sample
    rows = LIVE * members

    load_counts.wait()
    square = (total, total)
    diagonal = lax.broadcasted_iota(jnp.int32, square, 0) == lax.broadcasted_iota(jnp.int32, square, 1)
    for feature in range(held):
        level = counts_in[feature:feature + 1, :].astype(jnp.float32)
        column = jnp.sum(jnp.where(diagonal, level, 0.0), axis=1, keepdims=True)
        limits[feature] = jnp.broadcast_to(column, (total, LANES))

    for turn in range(groups):
        group = partner(turn)
        first = group * members

        def wait_ids(member):
            id_copy(first + member, first + member).wait_recv()

        if turn < groups - 1:
            @pl.loop(0, members, unroll=True)
            def _(member):
                wait_ids(member)
        else:
            @pl.loop(1, members, unroll=True)
            def _(step):
                wait_ids(lax.rem(dev + step, members))

        for feature in range(held):
            index = id_got[pl.ds(first, members), feature, :]
            high = jnp.where(on_lane, (index - (index & 15))[None], 0)
            low = jnp.where(on_lane, (index & 15)[None], 0)
            both = jnp.concatenate(
                [high.reshape(rows, LANES), low.reshape(rows, LANES)], axis=1
            ).astype(jnp.float32).astype(jnp.bfloat16)
            wide = jnp.dot(both, spread, preferred_element_type=jnp.float32)
            wide = wide.astype(jnp.int32).astype(jnp.int16)
            number = lax.broadcasted_iota(jnp.int32, (16, height), 1).astype(jnp.int16)
            for part in range(rows // 16):
                count = jnp.zeros((16, height), jnp.bfloat16)
                for entry in range(bagged):
                    piece = wide[part * 16:(part + 1) * 16, entry * LANES:(entry + 1) * LANES]
                    piece = jnp.concatenate([piece] * (height // LANES), axis=1)
                    count = count + jnp.where(
                        piece == number, jnp.ones((), jnp.bfloat16), jnp.zeros((), jnp.bfloat16)
                    )
                tally[part * 16:(part + 1) * 16, :] = count
            if turn == 0 and feature == 0:
                load_tables.wait()
            pooled = jnp.dot(
                tally[...], table_ref[feature], preferred_element_type=jnp.float32
            )
            limit = limits[feature, pl.ds(first, members), :]
            for half in range(halves):
                for s in range(LIVE):
                    piece = pooled[s * members:(s + 1) * members, half * LANES:(half + 1) * LANES]
                    line = (feature * halves + half) * LIVE + s
                    staged[pl.ds(line, members, stride=lines), :] = jnp.where(s < limit, piece, 0.0)
        outgoing[pl.ds(first, members)] = (
            staged[...].reshape(members, lines, LANES).astype(jnp.bfloat16)
        )

        if turn < groups - 1:
            @pl.loop(0, members, unroll=True)
            def _(step):
                row_copy(first + lax.rem(dev + step, members), me).start()
        else:
            @pl.loop(1, members, unroll=True)
            def _(step):
                row_copy(first + lax.rem(dev + step, members), me).start()

    @pl.loop(1, total, unroll=True)
    def _(step):
        id_copy(lax.rem(me + step, total), me).wait_send()

    received[me] = outgoing[me]
    out_ref[LIVE:] = jnp.zeros_like(out_ref[LIVE:])

    for turn in range(groups):
        if turn == groups - 1:
            @pl.loop(1, total, unroll=True)
            def _(step):
                row_copy(lax.rem(me + step, total), me).wait_send()

        group = origin(turn)
        first = group * members
        if turn < groups - 1:
            @pl.loop(0, members, unroll=True)
            def _(member):
                row_copy(first + member, first + member).wait_recv()
        else:
            @pl.loop(1, members, unroll=True)
            def _(step):
                source = first + lax.rem(dev + step, members)
                row_copy(source, source).wait_recv()
        staged[...] = (
            received[pl.ds(first, members)].astype(jnp.float32).reshape(members * lines, LANES)
        )
        for feature in range(held):
            for half in range(halves):
                for s in range(LIVE):
                    line = (feature * halves + half) * LIVE + s
                    vectors[s, half, group, pl.ds(feature, members, stride=held), :] = (
                        staged[pl.ds(line, members, stride=lines), :]
                    )

    for s in range(LIVE):
        mine = jnp.concatenate(
            [vectors[s, half].reshape(total * held, LANES) for half in range(halves)], axis=1
        ).astype(jnp.bfloat16)
        out_ref[s] = lax.dot_general(
            mine, mine, (((1,), (1,)), ((), ())), preferred_element_type=jnp.float32
        ).astype(jnp.bfloat16)


def shards(tables, ids, counts):
    held, height, width = tables.shape
    features, owned, bagged = ids.shape
    groups = lax.axis_size("node")
    members = lax.axis_size("dev")
    total = groups * members
    lines = held * (width // LANES) * LIVE
    index = ids.transpose(1, 2, 0).reshape(owned * bagged, features)
    return pl.pallas_call(
        functools.partial(kernel, groups, members, owned, bagged),
        out_shape=jax.ShapeDtypeStruct((owned, features, features), jnp.bfloat16),
        in_specs=[pl.BlockSpec(memory_space=pltpu.HBM)] * 3,
        out_specs=pl.BlockSpec(memory_space=pltpu.VMEM),
        scratch_shapes=[
            pltpu.VMEM(tables.shape, tables.dtype),
            pltpu.VMEM(index.shape, index.dtype),
            pltpu.VMEM(counts.shape, counts.dtype),
            pltpu.VMEM((total, held, LANES), jnp.int32),
            pltpu.VMEM((held, total, LANES), jnp.float32),
            pltpu.VMEM((total, held, LANES), jnp.int32),
            pltpu.VMEM((LIVE * members, height), jnp.bfloat16),
            pltpu.VMEM((members * lines, LANES), jnp.float32),
            pltpu.VMEM((total, lines, LANES), jnp.bfloat16),
            pltpu.VMEM((total, lines, LANES), jnp.bfloat16),
            pltpu.VMEM((LIVE, width // LANES, groups, members * held, LANES), jnp.float32),
            pltpu.SemaphoreType.DMA,
            pltpu.SemaphoreType.DMA,
            pltpu.SemaphoreType.DMA,
            pltpu.SemaphoreType.DMA((total,)),
            pltpu.SemaphoreType.DMA((total,)),
            pltpu.SemaphoreType.DMA((total,)),
            pltpu.SemaphoreType.DMA((total,)),
        ],
        compiler_params=pltpu.CompilerParams(
            collective_id=0, has_side_effects=True, vmem_limit_bytes=48 * 1024 * 1024
        ),
    )(*(pltpu.with_memory_space_constraint(x, pltpu.HBM) for x in (tables, index, counts)))


def solution(mesh):
    return jax.shard_map(
        shards,
        mesh=mesh,
        in_specs=(
            P(("node", "dev"), None, None),
            P(None, ("node", "dev"), None),
            P(("node", "dev"), None),
        ),
        out_specs=P(("node", "dev"), None, None),
        check_vma=False,
    )
```
